1024 devices in a mesh: band: 32 (over z_lo, y, core), ga: 32 (over z_hi, x).
Axes of the slice: x: 8, y: 8, z: 8 (z_hi: 4, z_lo: 2; z = z_hi * 2 + z_lo), core: 2. Of those that a mesh axis runs over, the one named last changes fastest.
Arguments:
- psi: float32 [1024, 196608], P('band', 'ga'), may hold values from -0.084712684 to 0.084712684
- hpsi: float32 [1024, 196608], P('band', 'ga'), may hold values from -6 to 6
Outputs:
- residual: float32 [1024, 196608], P('band', 'ga')
The draws below stay inside these ranges and needn't reach their ends.
All inputs are finite; a program needn't handle non-finite values.
Results may differ from the reference program's by a relative error of at most 0.0001.
Values sent between devices are 32-bit elements; how exact they have to be, the bound alone decides.
No kernel may reach another device: no remote copies, remote signals or barrier semaphores. Data moves between devices by JAX's collectives and lax.ppermute only.
A program may use at most 32 MiB of HBM per device.

```python
import jax
import jax.numpy as jnp
from jax import lax

BAND_DEV = 32
STEPS = 4
NB = 1024
NG = 196608
WINDOW = 128


def shard_levels(rng, extent, shards, smallest, high):
    def one(position, shards_of):
        steps = jax.random.uniform(jax.random.fold_in(jax.random.fold_in(rng, 6), position), (shards_of,), jnp.float32, smallest / len(shards), high / len(shards))
        return jnp.repeat(jnp.exp(steps), extent[position] // shards_of).reshape((-1,) + (1,) * (len(extent) - position - 1))

    factor_of = one(*shards[0])
    for cut in shards[1:]:
        factor_of = factor_of * one(*cut)
    return factor_of


def centred(stream_key, extent, scale, most, pieces=(), kind=jnp.bfloat16):
    factor_of = shard_levels(stream_key, extent, pieces, -0.22, 0.18) if pieces else 1.0
    result = jax.random.normal(stream_key, extent, jnp.float32) * scale * factor_of
    return jnp.minimum(jnp.maximum(result, -most), most).astype(kind)


def setup_inputs(seed: int = 0) -> dict:
    seeds = jax.random.split(jax.random.key(seed), 3)
    psi = centred(seeds[0], (NB, NG), ((WINDOW * NG) ** -0.25), 0.084712684, ((0, 32), (1, 32)), jnp.float32)
    hpsi = centred(seeds[1], (NB, NG), 1.0, 6.0, ((0, 32), (1, 32)), jnp.float32)
    return {"psi": psi, "hpsi": hpsi}


def reference(psi, hpsi):
    groups = NB // BAND_DEV
    psi_g = psi.reshape(groups, BAND_DEV, NG)
    hpsi_g = hpsi.reshape(groups, BAND_DEV, NG)
    total = jnp.zeros_like(hpsi_g)
    for k in range(STEPS):
        rolled = jnp.roll(psi_g, k, axis=0)
        intersection = jnp.einsum("bjg,big->bji", rolled, hpsi_g, precision=lax.Precision.HIGHEST)
        total = total + jnp.einsum("bji,bjg->big", intersection, rolled, precision=lax.Precision.HIGHEST)
    return (hpsi_g - total).reshape(NB, NG)
```

```python
import jax
import jax.numpy as jnp
from jax import lax
from jax.sharding import Mesh, PartitionSpec as P

BAND = ("zl", "y", "core")
GA = ("zh", "x")
PRECISION = lax.Precision.HIGH


def shifted(value, steps):
    count = lax.axis_size(BAND)
    pairs = [(source, (source + steps) % count) for source in range(count)]
    return lax.ppermute(value, BAND, pairs)


def swapped(value):
    return lax.ppermute(value, "core", [(0, 1), (1, 0)])


def overlap(h, psi):
    return lax.dot_general(
        h, psi, (((1,), (1,)), ((), ())), precision=PRECISION, preferred_element_type=jnp.float32
    )


def project(inter, psi):
    return lax.dot_general(
        inter, psi, (((1,), (0,)), ((), ())), precision=PRECISION, preferred_element_type=jnp.float32
    )


def summed(partial):
    count = lax.axis_size(GA)
    copies = jnp.broadcast_to(partial[None], (count,) + partial.shape)
    return jnp.sum(lax.all_to_all(copies, GA, 0, 0, tiled=True), 0)


def on_device(psi, hpsi):
    odd = lax.axis_index("core") == 1
    behind2 = shifted(psi, 2)
    ahead1 = shifted(hpsi, -1)
    for_next = jnp.concatenate([overlap(ahead1, psi), overlap(ahead1, behind2)], 1)
    from_previous = shifted(for_next, 1)
    own = jnp.concatenate([overlap(hpsi, psi), overlap(hpsi, behind2)], 1)
    inter = summed(jnp.concatenate([own, from_previous], 1))
    behind1 = swapped(jnp.where(odd, behind2, psi))
    behind3 = shifted(behind2, 1)
    window = jnp.concatenate([psi, behind2, behind1, behind3], 0)
    return hpsi - project(inter, window)


def solution(mesh):
    sizes = {"zl": 2, "y": 8, "core": 2, "zh": 4, "x": 8}
    fine = Mesh(mesh.devices.reshape(tuple(sizes.values())), tuple(sizes))
    placed = P(BAND, GA)
    return jax.shard_map(
        on_device, mesh=fine, in_specs=(placed, placed), out_specs=placed, check_vma=False
    )
```

```python
import jax
import jax.numpy as jnp
from jax import lax
from jax.experimental import pallas as pl
from jax.experimental.pallas import tpu as pltpu
from jax.sharding import Mesh, PartitionSpec as P

BAND = ("zl", "y", "core")
GA = ("zh", "x")
PRECISION = lax.Precision.HIGH


def shifted(value, steps, start=0, stride=1):
    count = lax.axis_size(BAND)
    pairs = [(source, (source + steps) % count) for source in range(start, count, stride)]
    return lax.ppermute(value, BAND, pairs)


def overlap(h, psi):
    return lax.dot_general(
        h, psi, (((1,), (1,)), ((), ())), precision=PRECISION, preferred_element_type=jnp.float32
    )


def folded(left, right):
    return jnp.concatenate([left[:16], left[16:], right[:16], right[16:]], 1)


def spread(block, count):
    return jnp.broadcast_to(block[None], (count,) + block.shape)


def halves(value):
    high = value.astype(jnp.bfloat16)
    return high, (value - high.astype(jnp.float32)).astype(jnp.bfloat16)


def product(left, right, dims):
    rows = left.shape[0]
    left_high, left_low = halves(left)
    right_high, right_low = halves(right)
    one = lax.dot_general(
        jnp.concatenate([left_high, left_low], 0),
        right_high,
        (dims, ((), ())),
        preferred_element_type=jnp.float32,
    )
    two = lax.dot_general(left_high, right_low, (dims, ((), ())), preferred_element_type=jnp.float32)
    return one[:rows] + one[rows:] + two


SCALAR = pl.BlockSpec(memory_space=pltpu.SMEM)
VECTOR = pl.BlockSpec(memory_space=pltpu.VMEM)
PARAMS = pltpu.CompilerParams(vmem_limit_bytes=40 << 20)


def near(*arrays):
    return [pltpu.with_memory_space_constraint(x, pltpu.VMEM) for x in arrays]


def slots_kernel(
    odd_ref, h_ref, a_ref, psi_ref, odd2_ref, even2_ref, own_ref, ahead_ref, own_odd_ref, hop_ref,
    out_ref, beside_ref, behind2_ref
):
    half = out_ref.shape[0] // 2

    def put(start, left, right):
        block = folded(left, right)
        for k in range(half):
            out_ref[start + k] = block

    step = h_ref.shape[1] // 4

    @pl.when(odd_ref[0] == 0)
    def _():
        late = jnp.zeros((64, 32), jnp.float32)
        for k in range(4):
            at = pl.ds(k * step, step)
            late += product(
                jnp.concatenate([h_ref[:, at], a_ref[:, at]], 0), even2_ref[:, at], ((1,), (1,))
            )
            beside_ref[:, at] = psi_ref[:, at]
            behind2_ref[:, at] = even2_ref[:, at]
        put(0, own_ref[...], late[:32])
        put(half, ahead_ref[...], late[32:])

    @pl.when(odd_ref[0] == 1)
    def _():
        put(0, hop_ref[:, :32], hop_ref[:, 32:])
        put(half, own_ref[...], own_odd_ref[...])
        for k in range(4):
            at = pl.ds(k * step, step)
            beside_ref[:, at] = odd2_ref[:, at]
            behind2_ref[:, at] = odd2_ref[:, at]


def slots_of(odd, wide, small, count):
    shape = pltpu.VMEM(wide[0].shape, jnp.float32)
    return pl.pallas_call(
        slots_kernel,
        out_shape=[pltpu.VMEM((count, 16, 128), jnp.float32), shape, shape],
        in_specs=[SCALAR] + [VECTOR] * 9,
        out_specs=[VECTOR] * 3,
        compiler_params=PARAMS,
    )(odd, *near(*wide, *small))


def line_kernel(got_ref, out_ref):
    half = got_ref.shape[0] // 2
    line = jnp.concatenate([jnp.sum(got_ref[:half], 0), jnp.sum(got_ref[half:], 0)], 0)
    for k in range(out_ref.shape[0]):
        out_ref[k] = line


def line_of(got, count):
    return pl.pallas_call(
        line_kernel,
        out_shape=pltpu.VMEM((count, 32, 128), jnp.float32),
        in_specs=[VECTOR],
        out_specs=VECTOR,
        cost_estimate=pl.CostEstimate(flops=5_000_000_000, bytes_accessed=1024, transcendentals=0),
    )(*near(got))


def finish_kernel(
    odd_ref, got_ref, psi_ref, behind2_ref, behind3_ref, behind1_ref, h_ref,
    out_ref, h, made, into, out
):
    steps = into.shape[0]
    step = h.shape[1] // steps
    loads = []
    for k in range(steps):
        at = pl.ds(k * step, step)
        loads.append(pltpu.make_async_copy(h_ref.at[:, at], h.at[:, at], into.at[k]))
        loads[-1].start()

    total = jnp.sum(got_ref[...], 0)
    odd = odd_ref[0] == 1
    own = jnp.where(odd, total[16:], total[:16])
    ahead = jnp.where(odd, total[:16], total[16:])

    def unfolded(block):
        return [
            jnp.concatenate([block[:, k : k + 32], block[:, k + 32 : k + 64]], 0) for k in (0, 64)
        ]

    mine, next_to = unfolded(own), unfolded(ahead)
    high, low = halves(jnp.concatenate(mine + next_to[::-1], 1))
    both = jnp.concatenate([high, low], 0)

    def times(left, right):
        return lax.dot_general(
            left, right, (((1,), (0,)), ((), ())), preferred_element_type=jnp.float32
        )

    stores = []
    for k in range(steps):
        at = pl.ds(k * step, step)
        blocks = [ref[:, at] for ref in (psi_ref, behind2_ref, behind3_ref, behind1_ref)]
        window_high, window_low = halves(jnp.concatenate(blocks, 0))
        one, two = times(both, window_high), times(high, window_low)
        loads[k].wait()
        made[:, at] = h[:, at] - (one[:32] + one[32:] + two)
        stores.append(pltpu.make_async_copy(made.at[:, at], out_ref.at[:, at], out.at[k]))
        stores[-1].start()
    for copy in stores:
        copy.wait()


def finished(odd, got, window, hpsi):
    block = pltpu.VMEM(hpsi.shape, jnp.float32)
    return pl.pallas_call(
        finish_kernel,
        out_shape=jax.ShapeDtypeStruct(hpsi.shape, jnp.float32),
        in_specs=[SCALAR] + [VECTOR] * 5 + [pl.BlockSpec(memory_space=pl.ANY)],
        out_specs=pl.BlockSpec(memory_space=pl.ANY),
        scratch_shapes=[block, block, pltpu.SemaphoreType.DMA((6,)), pltpu.SemaphoreType.DMA((6,))],
        compiler_params=PARAMS,
    )(odd, *near(got, *window), hpsi)


def on_device(psi, hpsi):
    core = lax.axis_index("core")
    odd = core.astype(jnp.int32).reshape(1)
    odd2 = shifted(psi, 2, 1, 2)
    ahead1 = shifted(hpsi, -1)
    own, own_odd = overlap(hpsi, psi), overlap(hpsi, odd2)
    psi_later, own, own_odd = lax.optimization_barrier((psi, own, own_odd))
    even2 = shifted(psi_later, 2, 0, 2)

    ahead, ahead_odd = overlap(ahead1, psi), overlap(ahead1, odd2)
    hopped = shifted(jnp.concatenate([ahead, ahead_odd], 1), 2, 1, 2)

    slots, beside, behind2 = slots_of(
        odd,
        (hpsi, ahead1, psi, odd2, even2),
        (own, ahead, own_odd, hopped),
        2 * lax.axis_size("x"),
    )
    got = lax.all_to_all(slots, ("core", "x"), 0, 0, tiled=True)
    line = line_of(got, lax.axis_size("zh"))
    behind3 = shifted(behind2, 1)
    behind1 = lax.ppermute(beside, "core", [(0, 1), (1, 0)])
    got = lax.all_to_all(line, "zh", 0, 0, tiled=True)
    return finished(odd, got, (psi, behind2, behind3, behind1), hpsi)


def solution(mesh):
    sizes = {"zl": 2, "y": 8, "core": 2, "zh": 4, "x": 8}
    fine = Mesh(mesh.devices.reshape(tuple(sizes.values())), tuple(sizes))
    placed = P(BAND, GA)
    return jax.shard_map(
        on_device, mesh=fine, in_specs=(placed, placed), out_specs=placed, check_vma=False
    )
```

```python
import jax
import jax.numpy as jnp
from jax import lax
from jax.experimental import pallas as pl
from jax.experimental.pallas import tpu as pltpu
from jax.sharding import Mesh, PartitionSpec as P

BAND = ("zl", "y", "core")
GA = ("zh", "x")
PRECISION = lax.Precision.HIGH


def shifted(value, steps, start=0, stride=1):
    count = lax.axis_size(BAND)
    pairs = [(source, (source + steps) % count) for source in range(start, count, stride)]
    return lax.ppermute(value, BAND, pairs)


def overlap(h, psi):
    return lax.dot_general(
        h, psi, (((1,), (1,)), ((), ())), precision=PRECISION, preferred_element_type=jnp.float32
    )


def folded(left, right):
    return jnp.concatenate([left[:16], left[16:], right[:16], right[16:]], 1)


def spread(block, count):
    return jnp.broadcast_to(block[None], (count,) + block.shape)


def halves(value):
    high = value.astype(jnp.bfloat16)
    return high, (value - high.astype(jnp.float32)).astype(jnp.bfloat16)


def product(left, right, dims):
    rows = left.shape[0]
    left_high, left_low = halves(left)
    right_high, right_low = halves(right)
    one = lax.dot_general(
        jnp.concatenate([left_high, left_low], 0),
        right_high,
        (dims, ((), ())),
        preferred_element_type=jnp.float32,
    )
    two = lax.dot_general(left_high, right_low, (dims, ((), ())), preferred_element_type=jnp.float32)
    return one[:rows] + one[rows:] + two


SCALAR = pl.BlockSpec(memory_space=pltpu.SMEM)
VECTOR = pl.BlockSpec(memory_space=pltpu.VMEM)
PARAMS = pltpu.CompilerParams(vmem_limit_bytes=40 << 20)


def near(*arrays):
    return [pltpu.with_memory_space_constraint(x, pltpu.VMEM) for x in arrays]


def slots_kernel(odd_ref, h_ref, a_ref, even_ref, own_ref, ahead_ref, own_odd_ref, hop_ref, out_ref):
    half = out_ref.shape[0] // 2

    def put(start, left, right):
        block = folded(left, right)
        for k in range(half):
            out_ref[start + k] = block

    @pl.when(odd_ref[0] == 0)
    def _():
        step = h_ref.shape[1] // 4
        late = jnp.zeros((64, 32), jnp.float32)
        for k in range(4):
            at = pl.ds(k * step, step)
            late += product(
                jnp.concatenate([h_ref[:, at], a_ref[:, at]], 0), even_ref[:, at], ((1,), (1,))
            )
        put(0, own_ref[...], late[:32])
        put(half, ahead_ref[...], late[32:])

    @pl.when(odd_ref[0] == 1)
    def _():
        put(0, hop_ref[:, :32], hop_ref[:, 32:])
        put(half, own_ref[...], own_odd_ref[...])


def slots_of(odd, wide, small, count):
    return pl.pallas_call(
        slots_kernel,
        out_shape=jax.ShapeDtypeStruct((count, 16, 128), jnp.float32),
        in_specs=[SCALAR] + [VECTOR] * 7,
        out_specs=VECTOR,
        compiler_params=PARAMS,
    )(odd, *near(*wide), *small)


def line_kernel(got_ref, out_ref):
    half = got_ref.shape[0] // 2
    line = jnp.concatenate([jnp.sum(got_ref[:half], 0), jnp.sum(got_ref[half:], 0)], 0)
    for k in range(out_ref.shape[0]):
        out_ref[k] = line


def line_of(got, count):
    return pl.pallas_call(
        line_kernel,
        out_shape=pltpu.VMEM((count, 32, 128), jnp.float32),
        in_specs=[VECTOR],
        out_specs=VECTOR,
        cost_estimate=pl.CostEstimate(flops=5_000_000_000, bytes_accessed=1024, transcendentals=0),
    )(*near(got))


def total_kernel(odd_ref, got_ref, out_ref):
    total = jnp.sum(got_ref[...], 0)
    odd = odd_ref[0] == 1
    own = jnp.where(odd, total[16:], total[:16])
    ahead = jnp.where(odd, total[:16], total[16:])
    for n, block in enumerate((own, ahead)):
        for k in range(2):
            rows = [block[:, 64 * k + 32 * r : 64 * k + 32 * r + 32] for r in range(2)]
            out_ref[:, 64 * n + 32 * k : 64 * n + 32 * k + 32] = jnp.concatenate(rows, 0)


def total_of(odd, got):
    return pl.pallas_call(
        total_kernel,
        out_shape=pltpu.VMEM((32, 128), jnp.float32),
        in_specs=[SCALAR, VECTOR],
        out_specs=VECTOR,
        cost_estimate=pl.CostEstimate(
            flops=5_000_000_000, bytes_accessed=1024, transcendentals=0
        ),
    )(odd, *near(got))


def finish_kernel(
    odd_ref, inter_ref, psi_ref, odd1_ref, even1_ref, odd2_ref, even2_ref, odd3_ref, even3_ref, h_ref,
    out_ref, h, made, into, out
):
    steps = into.shape[0]
    step = h.shape[1] // steps
    loads = []
    for k in range(steps):
        at = pl.ds(k * step, step)
        loads.append(pltpu.make_async_copy(h_ref.at[:, at], h.at[:, at], into.at[k]))
        loads[-1].start()
    inter = inter_ref[...]

    def finish(*behind):
        stores = []
        for k in range(steps):
            at = pl.ds(k * step, step)
            window = jnp.concatenate([ref[:, at] for ref in (psi_ref,) + behind], 0)
            shift = product(inter, window, ((1,), (0,)))
            loads[k].wait()
            made[:, at] = h[:, at] - shift
            stores.append(pltpu.make_async_copy(made.at[:, at], out_ref.at[:, at], out.at[k]))
            stores[-1].start()
        for copy in stores:
            copy.wait()

    @pl.when(odd_ref[0] == 0)
    def _():
        finish(even2_ref, odd1_ref, odd3_ref)

    @pl.when(odd_ref[0] == 1)
    def _():
        finish(odd2_ref, even1_ref, even3_ref)


def finished(odd, inter, blocks, hpsi):
    block = pltpu.VMEM(hpsi.shape, jnp.float32)
    return pl.pallas_call(
        finish_kernel,
        out_shape=jax.ShapeDtypeStruct(hpsi.shape, jnp.float32),
        in_specs=[SCALAR] + [VECTOR] * 8 + [pl.BlockSpec(memory_space=pl.ANY)],
        out_specs=pl.BlockSpec(memory_space=pl.ANY),
        scratch_shapes=[block, block, pltpu.SemaphoreType.DMA((6,)), pltpu.SemaphoreType.DMA((6,))],
        compiler_params=PARAMS,
    )(odd, *near(inter, *blocks), hpsi)


def on_device(psi, hpsi):
    odd = lax.axis_index("core").astype(jnp.int32).reshape(1)
    odd2 = shifted(psi, 2, 1, 2)
    ahead1 = shifted(hpsi, -1)
    own, own_odd = overlap(hpsi, psi), overlap(hpsi, odd2)
    psi_later, own, own_odd = lax.optimization_barrier((psi, own, own_odd))
    even2 = shifted(psi_later, 2, 0, 2)

    ahead, ahead_odd = overlap(ahead1, psi), overlap(ahead1, odd2)
    hopped = shifted(jnp.concatenate([ahead, ahead_odd], 1), 2, 1, 2)
    even1 = lax.ppermute(psi, "core", [(0, 1)])

    slots = slots_of(
        odd, (hpsi, ahead1, even2), (own, ahead, own_odd, hopped), 2 * lax.axis_size("x")
    )
    slots, odd2_later = lax.optimization_barrier((slots, odd2))
    got = lax.all_to_all(slots, ("core", "x"), 0, 0, tiled=True)
    odd3 = shifted(odd2_later, 1, 1, 2)
    line = line_of(got, lax.axis_size("zh"))
    line, odd2_last, even2_last = lax.optimization_barrier((line, odd2, even2))
    got = lax.all_to_all(line, "zh", 0, 0, tiled=True)
    odd1 = lax.ppermute(odd2_last, "core", [(1, 0)])
    even3 = lax.ppermute(even2_last, "core", [(0, 1)])
    inter = total_of(odd, got)
    return finished(odd, inter, (psi, odd1, even1, odd2, even2, odd3, even3), hpsi)


def solution(mesh):
    sizes = {"zl": 2, "y": 8, "core": 2, "zh": 4, "x": 8}
    fine = Mesh(mesh.devices.reshape(tuple(sizes.values())), tuple(sizes))
    placed = P(BAND, GA)
    return jax.shard_map(
        on_device, mesh=fine, in_specs=(placed, placed), out_specs=placed, check_vma=False
    )
```

```python
import jax
import jax.numpy as jnp
from jax import lax
from jax.experimental import pallas as pl
from jax.experimental.pallas import tpu as pltpu
from jax.sharding import Mesh, PartitionSpec as P

BAND = ("zl", "y", "core")
GA = ("zh", "x")
PRECISION = lax.Precision.HIGH


def shifted(value, steps, start=0, stride=1):
    count = lax.axis_size(BAND)
    pairs = [(source, (source + steps) % count) for source in range(start, count, stride)]
    return lax.ppermute(value, BAND, pairs)


def overlap(h, psi):
    return lax.dot_general(
        h, psi, (((1,), (1,)), ((), ())), precision=PRECISION, preferred_element_type=jnp.float32
    )


def folded(left, right):
    return jnp.concatenate([left[:16], left[16:], right[:16], right[16:]], 1)


def spread(block, count):
    return jnp.broadcast_to(block[None], (count,) + block.shape)


def halves(value):
    high = value.astype(jnp.bfloat16)
    return high, (value - high.astype(jnp.float32)).astype(jnp.bfloat16)


def product(left, right, dims):
    rows = left.shape[0]
    left_high, left_low = halves(left)
    right_high, right_low = halves(right)
    one = lax.dot_general(
        jnp.concatenate([left_high, left_low], 0),
        right_high,
        (dims, ((), ())),
        preferred_element_type=jnp.float32,
    )
    two = lax.dot_general(left_high, right_low, (dims, ((), ())), preferred_element_type=jnp.float32)
    return one[:rows] + one[rows:] + two


SCALAR = pl.BlockSpec(memory_space=pltpu.SMEM)
VECTOR = pl.BlockSpec(memory_space=pltpu.VMEM)
ANYWHERE = pl.BlockSpec(memory_space=pl.ANY)
PARAMS = pltpu.CompilerParams(vmem_limit_bytes=40 << 20)


def near(*arrays):
    return [pltpu.with_memory_space_constraint(x, pltpu.VMEM) for x in arrays]


def slots_kernel(
    odd_ref, h_ref, a_ref, even_ref, own_ref, ahead_ref, own_odd_ref, hop_ref, out_ref, wide, sems
):
    half = out_ref.shape[0] // 2

    def put(start, left, right):
        block = folded(left, right)
        for k in range(half):
            out_ref[start + k] = block

    @pl.when(odd_ref[0] == 0)
    def _():
        steps = sems.shape[0]
        step = wide.shape[2] // steps
        spans = [pl.ds(k * step, step) for k in range(steps)]
        loads = [
            [
                pltpu.make_async_copy(ref.at[:, at], wide.at[n, :, at], sems.at[k, n])
                for n, ref in enumerate((h_ref, a_ref, even_ref))
            ]
            for k, at in enumerate(spans)
        ]
        for load in loads:
            for copy in load:
                copy.start()
        late = jnp.zeros((64, 32), jnp.float32)
        for load, at in zip(loads, spans):
            for copy in load:
                copy.wait()
            left = jnp.concatenate([wide[0, :, at], wide[1, :, at]], 0)
            late += product(left, wide[2, :, at], ((1,), (1,)))
        put(0, own_ref[...], late[:32])
        put(half, ahead_ref[...], late[32:])

    @pl.when(odd_ref[0] == 1)
    def _():
        put(0, hop_ref[:, :32], hop_ref[:, 32:])
        put(half, own_ref[...], own_odd_ref[...])


def slots_of(odd, wide, small, count):
    return pl.pallas_call(
        slots_kernel,
        out_shape=jax.ShapeDtypeStruct((count, 16, 128), jnp.float32),
        in_specs=[SCALAR] + [ANYWHERE] * 3 + [VECTOR] * 4,
        out_specs=VECTOR,
        scratch_shapes=[
            pltpu.VMEM((3,) + wide[0].shape, jnp.float32),
            pltpu.SemaphoreType.DMA((4, 3)),
        ],
        compiler_params=PARAMS,
    )(odd, *near(*wide), *small)


def line_kernel(got_ref, out_ref):
    half = got_ref.shape[0] // 2
    line = jnp.concatenate([jnp.sum(got_ref[:half], 0), jnp.sum(got_ref[half:], 0)], 0)
    for k in range(out_ref.shape[0]):
        out_ref[k] = line


def line_of(got, count):
    return pl.pallas_call(
        line_kernel,
        out_shape=pltpu.VMEM((count, 32, 128), jnp.float32),
        in_specs=[VECTOR],
        out_specs=VECTOR,
        cost_estimate=pl.CostEstimate(flops=5_000_000_000, bytes_accessed=1024, transcendentals=0),
    )(*near(got))


def total_kernel(odd_ref, got_ref, out_ref):
    total = jnp.sum(got_ref[...], 0)
    odd = odd_ref[0] == 1
    own = jnp.where(odd, total[16:], total[:16])
    ahead = jnp.where(odd, total[:16], total[16:])
    for n, block in enumerate((own, ahead)):
        for k in range(2):
            rows = [block[:, 64 * k + 32 * r : 64 * k + 32 * r + 32] for r in range(2)]
            out_ref[:, 64 * n + 32 * k : 64 * n + 32 * k + 32] = jnp.concatenate(rows, 0)


def total_of(odd, got):
    return pl.pallas_call(
        total_kernel,
        out_shape=pltpu.VMEM((32, 128), jnp.float32),
        in_specs=[SCALAR, VECTOR],
        out_specs=VECTOR,
        cost_estimate=pl.CostEstimate(
            flops=8_000_000_000, bytes_accessed=1024, transcendentals=0
        ),
    )(odd, *near(got))


def finish_kernel(
    odd_ref, inter_ref, psi_ref, odd1_ref, even1_ref, odd2_ref, even2_ref, odd3_ref, even3_ref, h_ref,
    out_ref, wide, made, into, out
):
    steps = out.shape[0]
    step = made.shape[1] // steps
    spans = [pl.ds(k * step, step) for k in range(steps)]

    def finish(*refs):
        loads = [
            [
                pltpu.make_async_copy(ref.at[:, at], wide.at[n, :, at], into.at[k, n])
                for n, ref in enumerate(refs)
            ]
            for k, at in enumerate(spans)
        ]
        for load in loads:
            for copy in load:
                copy.start()
        inter = inter_ref[...]
        stores = []
        for k, at in enumerate(spans):
            for copy in loads[k]:
                copy.wait()
            window = jnp.concatenate([wide[n, :, at] for n in range(1, 5)], 0)
            made[:, at] = wide[0, :, at] - product(inter, window, ((1,), (0,)))
            stores.append(pltpu.make_async_copy(made.at[:, at], out_ref.at[:, at], out.at[k]))
            stores[-1].start()
        for copy in stores:
            copy.wait()

    @pl.when(odd_ref[0] == 0)
    def _():
        finish(h_ref, psi_ref, even2_ref, odd1_ref, odd3_ref)

    @pl.when(odd_ref[0] == 1)
    def _():
        finish(h_ref, psi_ref, odd2_ref, even1_ref, even3_ref)


def finished(odd, inter, blocks, hpsi):
    shape = hpsi.shape
    return pl.pallas_call(
        finish_kernel,
        out_shape=jax.ShapeDtypeStruct(shape, jnp.float32),
        in_specs=[SCALAR, VECTOR] + [ANYWHERE] * 8,
        out_specs=ANYWHERE,
        scratch_shapes=[
            pltpu.VMEM((5,) + shape, jnp.float32),
            pltpu.VMEM(shape, jnp.float32),
            pltpu.SemaphoreType.DMA((6, 5)),
            pltpu.SemaphoreType.DMA((6,)),
        ],
        compiler_params=PARAMS,
    )(odd, *near(inter, *blocks), hpsi)


def on_device(psi, hpsi):
    odd = lax.axis_index("core").astype(jnp.int32).reshape(1)
    odd2 = shifted(psi, 2, 1, 2)
    ahead1 = shifted(hpsi, -1)
    own, own_odd = overlap(hpsi, psi), overlap(hpsi, odd2)
    psi_later, own, own_odd = lax.optimization_barrier((psi, own, own_odd))
    even2 = shifted(psi_later, 2, 0, 2)

    ahead, ahead_odd = overlap(ahead1, psi), overlap(ahead1, odd2)
    hopped = shifted(jnp.concatenate([ahead, ahead_odd], 1), 2, 1, 2)
    even1 = lax.ppermute(psi, "core", [(0, 1)])

    slots = slots_of(
        odd, (hpsi, ahead1, even2), (own, ahead, own_odd, hopped), 2 * lax.axis_size("x")
    )
    slots, odd2_later = lax.optimization_barrier((slots, odd2))
    got = lax.all_to_all(slots, ("core", "x"), 0, 0, tiled=True)
    odd3 = shifted(odd2_later, 1, 1, 2)
    line = line_of(got, lax.axis_size("zh"))
    line, odd2_last, even2_last = lax.optimization_barrier((line, odd2, even2))
    got = lax.all_to_all(line, "zh", 0, 0, tiled=True)
    odd1 = lax.ppermute(odd2_last, "core", [(1, 0)])
    even3 = lax.ppermute(even2_last, "core", [(0, 1)])
    got, odd3, even1 = lax.optimization_barrier((got, odd3, even1))
    inter = total_of(odd, got)
    return finished(odd, inter, (psi, odd1, even1, odd2, even2, odd3, even3), hpsi)


def solution(mesh):
    sizes = {"zl": 2, "y": 8, "core": 2, "zh": 4, "x": 8}
    fine = Mesh(mesh.devices.reshape(tuple(sizes.values())), tuple(sizes))
    placed = P(BAND, GA)
    return jax.shard_map(
        on_device, mesh=fine, in_specs=(placed, placed), out_specs=placed, check_vma=False
    )
```

```python
import jax
import jax.numpy as jnp
from jax import lax
from jax.experimental import pallas as pl
from jax.experimental.pallas import tpu as pltpu
from jax.sharding import Mesh, PartitionSpec as P

BAND = ("zl", "y", "core")
GA = ("zh", "x")
PRECISION = lax.Precision.HIGH


def shifted(value, steps, start=0, stride=1):
    count = lax.axis_size(BAND)
    pairs = [(source, (source + steps) % count) for source in range(start, count, stride)]
    return lax.ppermute(value, BAND, pairs)


def overlap(h, psi):
    return lax.dot_general(
        h, psi, (((1,), (1,)), ((), ())), precision=PRECISION, preferred_element_type=jnp.float32
    )


def folded(left, right):
    return jnp.concatenate([left[:16], left[16:], right[:16], right[16:]], 1)


def spread(block, count):
    return jnp.broadcast_to(block[None], (count,) + block.shape)


def halves(value):
    high = value.astype(jnp.bfloat16)
    return high, (value - high.astype(jnp.float32)).astype(jnp.bfloat16)


def product(left, right, dims):
    rows = left.shape[0]
    left_high, left_low = halves(left)
    right_high, right_low = halves(right)
    one = lax.dot_general(
        jnp.concatenate([left_high, left_low], 0),
        right_high,
        (dims, ((), ())),
        preferred_element_type=jnp.float32,
    )
    two = lax.dot_general(left_high, right_low, (dims, ((), ())), preferred_element_type=jnp.float32)
    return one[:rows] + one[rows:] + two


SCALAR = pl.BlockSpec(memory_space=pltpu.SMEM)
VECTOR = pl.BlockSpec(memory_space=pltpu.VMEM)
ANYWHERE = pl.BlockSpec(memory_space=pl.ANY)
PARAMS = pltpu.CompilerParams(vmem_limit_bytes=40 << 20)


def near(*arrays):
    return [pltpu.with_memory_space_constraint(x, pltpu.VMEM) for x in arrays]


def slots_kernel(
    odd_ref, h_ref, a_ref, even_ref, own_ref, ahead_ref, own_odd_ref, hop_ref, out_ref, late_ref, sems
):
    half = out_ref.shape[0] // 2

    def put(start, left, right):
        block = folded(left, right)
        for k in range(half):
            out_ref[start + k] = block

    @pl.when(odd_ref[0] == 0)
    def _():
        steps = sems.shape[0]
        step = late_ref.shape[1] // steps
        spans = [pl.ds(k * step, step) for k in range(steps)]
        loads = [
            pltpu.make_async_copy(even_ref.at[:, at], late_ref.at[:, at], sems.at[k])
            for k, at in enumerate(spans)
        ]
        for load in loads:
            load.start()
        late = jnp.zeros((64, 32), jnp.float32)
        for load, at in zip(loads, spans):
            load.wait()
            left = jnp.concatenate([h_ref[:, at], a_ref[:, at]], 0)
            late += product(left, late_ref[:, at], ((1,), (1,)))
        put(0, own_ref[...], late[:32])
        put(half, ahead_ref[...], late[32:])

    @pl.when(odd_ref[0] == 1)
    def _():
        put(0, hop_ref[:, :32], hop_ref[:, 32:])
        put(half, own_ref[...], own_odd_ref[...])


def slots_of(odd, wide, small, count):
    return pl.pallas_call(
        slots_kernel,
        out_shape=jax.ShapeDtypeStruct((count, 16, 128), jnp.float32),
        in_specs=[SCALAR, VECTOR, VECTOR, ANYWHERE] + [VECTOR] * 4,
        out_specs=VECTOR,
        scratch_shapes=[
            pltpu.VMEM(wide[0].shape, jnp.float32),
            pltpu.SemaphoreType.DMA((4,)),
        ],
        compiler_params=PARAMS,
    )(odd, *near(*wide), *small)


def line_kernel(got_ref, out_ref):
    half = got_ref.shape[0] // 2
    line = jnp.concatenate([jnp.sum(got_ref[:half], 0), jnp.sum(got_ref[half:], 0)], 0)
    for k in range(out_ref.shape[0]):
        out_ref[k] = line


def line_of(got, count):
    return pl.pallas_call(
        line_kernel,
        out_shape=pltpu.VMEM((count, 32, 128), jnp.float32),
        in_specs=[VECTOR],
        out_specs=VECTOR,
        cost_estimate=pl.CostEstimate(flops=5_000_000_000, bytes_accessed=1024, transcendentals=0),
    )(*near(got))


def total_kernel(odd_ref, got_ref, out_ref):
    total = jnp.sum(got_ref[...], 0)
    odd = odd_ref[0] == 1
    own = jnp.where(odd, total[16:], total[:16])
    ahead = jnp.where(odd, total[:16], total[16:])
    for n, block in enumerate((own, ahead)):
        for k in range(2):
            rows = [block[:, 64 * k + 32 * r : 64 * k + 32 * r + 32] for r in range(2)]
            out_ref[:, 64 * n + 32 * k : 64 * n + 32 * k + 32] = jnp.concatenate(rows, 0)


def total_of(odd, got):
    return pl.pallas_call(
        total_kernel,
        out_shape=pltpu.VMEM((32, 128), jnp.float32),
        in_specs=[SCALAR, VECTOR],
        out_specs=VECTOR,
        cost_estimate=pl.CostEstimate(
            flops=8_000_000_000, bytes_accessed=1024, transcendentals=0
        ),
    )(odd, *near(got))


def finish_kernel(
    odd_ref, inter_ref, psi_ref, odd1_ref, even1_ref, odd2_ref, even2_ref, odd3_ref, even3_ref, h_ref,
    out_ref, wide, made, into, out
):
    steps = out.shape[0]
    step = made.shape[1] // steps
    spans = [pl.ds(k * step, step) for k in range(steps)]

    def finish(*refs):
        loads = [
            [
                pltpu.make_async_copy(ref.at[:, at], wide.at[n, :, at], into.at[k, n])
                for n, ref in enumerate(refs)
            ]
            for k, at in enumerate(spans)
        ]
        for load in loads:
            for copy in load:
                copy.start()
        inter = inter_ref[...]
        stores = []
        for k, at in enumerate(spans):
            for copy in loads[k]:
                copy.wait()
            window = jnp.concatenate([wide[n, :, at] for n in range(1, 5)], 0)
            made[:, at] = wide[0, :, at] - product(inter, window, ((1,), (0,)))
            stores.append(pltpu.make_async_copy(made.at[:, at], out_ref.at[:, at], out.at[k]))
            stores[-1].start()
        for copy in stores:
            copy.wait()

    @pl.when(odd_ref[0] == 0)
    def _():
        finish(h_ref, psi_ref, even2_ref, odd1_ref, odd3_ref)

    @pl.when(odd_ref[0] == 1)
    def _():
        finish(h_ref, psi_ref, odd2_ref, even1_ref, even3_ref)


def finished(odd, inter, blocks, hpsi):
    shape = hpsi.shape
    return pl.pallas_call(
        finish_kernel,
        out_shape=jax.ShapeDtypeStruct(shape, jnp.float32),
        in_specs=[SCALAR, VECTOR] + [ANYWHERE] * 8,
        out_specs=ANYWHERE,
        scratch_shapes=[
            pltpu.VMEM((5,) + shape, jnp.float32),
            pltpu.VMEM(shape, jnp.float32),
            pltpu.SemaphoreType.DMA((6, 5)),
            pltpu.SemaphoreType.DMA((6,)),
        ],
        compiler_params=PARAMS,
    )(odd, *near(inter, *blocks), hpsi)


def on_device(psi, hpsi):
    odd = lax.axis_index("core").astype(jnp.int32).reshape(1)
    odd2 = shifted(psi, 2, 1, 2)
    ahead1 = shifted(hpsi, -1)
    own, own_odd = overlap(hpsi, psi), overlap(hpsi, odd2)
    psi_later, own, own_odd = lax.optimization_barrier((psi, own, own_odd))
    even2 = shifted(psi_later, 2, 0, 2)

    ahead, ahead_odd = overlap(ahead1, psi), overlap(ahead1, odd2)
    hopped = shifted(jnp.concatenate([ahead, ahead_odd], 1), 2, 1, 2)

    slots = slots_of(
        odd, (hpsi, ahead1, even2), (own, ahead, own_odd, hopped), 2 * lax.axis_size("x")
    )
    slots, odd2_later, psi_later = lax.optimization_barrier((slots, odd2, psi))
    got = lax.all_to_all(slots, ("core", "x"), 0, 0, tiled=True)
    odd3 = shifted(odd2_later, 1, 1, 2)
    even1 = lax.ppermute(psi_later, "core", [(0, 1)])
    line = line_of(got, lax.axis_size("zh"))
    line, odd2_last, even2_last = lax.optimization_barrier((line, odd2, even2))
    got = lax.all_to_all(line, "zh", 0, 0, tiled=True)
    odd1 = lax.ppermute(odd2_last, "core", [(1, 0)])
    even3 = lax.ppermute(even2_last, "core", [(0, 1)])
    got, odd3 = lax.optimization_barrier((got, odd3))
    got, even1 = lax.optimization_barrier((got, even1))
    inter = total_of(odd, got)
    return finished(odd, inter, (psi, odd1, even1, odd2, even2, odd3, even3), hpsi)


def solution(mesh):
    sizes = {"zl": 2, "y": 8, "core": 2, "zh": 4, "x": 8}
    fine = Mesh(mesh.devices.reshape(tuple(sizes.values())), tuple(sizes))
    placed = P(BAND, GA)
    return jax.shard_map(
        on_device, mesh=fine, in_specs=(placed, placed), out_specs=placed, check_vma=False
    )
```

```python
import jax
import jax.numpy as jnp
from jax import lax
from jax.experimental import pallas as pl
from jax.experimental.pallas import tpu as pltpu
from jax.sharding import Mesh, PartitionSpec as P

BAND = ("zl", "y", "core")
GA = ("zh", "x")
PRECISION = lax.Precision.HIGH


def shifted(value, steps, start=0, stride=1):
    count = lax.axis_size(BAND)
    pairs = [(source, (source + steps) % count) for source in range(start, count, stride)]
    return lax.ppermute(value, BAND, pairs)


def overlap(h, psi):
    return lax.dot_general(
        h, psi, (((1,), (1,)), ((), ())), precision=PRECISION, preferred_element_type=jnp.float32
    )


def folded(left, right):
    return jnp.concatenate([left[:16], left[16:], right[:16], right[16:]], 1)


def spread(block, count):
    return jnp.broadcast_to(block[None], (count,) + block.shape)


def halves(value):
    high = value.astype(jnp.bfloat16)
    return high, (value - high.astype(jnp.float32)).astype(jnp.bfloat16)


def product(left, right, dims):
    rows = left.shape[0]
    left_high, left_low = halves(left)
    right_high, right_low = halves(right)
    one = lax.dot_general(
        jnp.concatenate([left_high, left_low], 0),
        right_high,
        (dims, ((), ())),
        preferred_element_type=jnp.float32,
    )
    two = lax.dot_general(left_high, right_low, (dims, ((), ())), preferred_element_type=jnp.float32)
    return one[:rows] + one[rows:] + two


SCALAR = pl.BlockSpec(memory_space=pltpu.SMEM)
VECTOR = pl.BlockSpec(memory_space=pltpu.VMEM)
ANYWHERE = pl.BlockSpec(memory_space=pl.ANY)
PARAMS = pltpu.CompilerParams(vmem_limit_bytes=40 << 20)


def near(*arrays):
    return [pltpu.with_memory_space_constraint(x, pltpu.VMEM) for x in arrays]


def slots_kernel(
    odd_ref, h_ref, a_ref, even_ref, own_ref, ahead_ref, own_odd_ref, hop_ref, out_ref, late_ref, sems
):
    half = out_ref.shape[0] // 2

    def put(start, left, right):
        block = folded(left, right)
        for k in range(half):
            out_ref[start + k] = block

    @pl.when(odd_ref[0] == 0)
    def _():
        steps = sems.shape[0]
        step = late_ref.shape[1] // steps
        spans = [pl.ds(k * step, step) for k in range(steps)]
        loads = [
            pltpu.make_async_copy(even_ref.at[:, at], late_ref.at[:, at], sems.at[k])
            for k, at in enumerate(spans)
        ]
        for load in loads:
            load.start()
        late = jnp.zeros((64, 32), jnp.float32)
        for load, at in zip(loads, spans):
            load.wait()
            left = jnp.concatenate([h_ref[:, at], a_ref[:, at]], 0)
            late += product(left, late_ref[:, at], ((1,), (1,)))
        put(0, own_ref[...], late[:32])
        put(half, ahead_ref[...], late[32:])

    @pl.when(odd_ref[0] == 1)
    def _():
        put(0, hop_ref[:, :32], hop_ref[:, 32:])
        put(half, own_ref[...], own_odd_ref[...])


def slots_of(odd, wide, small, count):
    return pl.pallas_call(
        slots_kernel,
        out_shape=jax.ShapeDtypeStruct((count, 16, 128), jnp.float32),
        in_specs=[SCALAR, VECTOR, VECTOR, ANYWHERE] + [VECTOR] * 4,
        out_specs=VECTOR,
        scratch_shapes=[
            pltpu.VMEM(wide[0].shape, jnp.float32),
            pltpu.SemaphoreType.DMA((4,)),
        ],
        compiler_params=PARAMS,
    )(odd, *near(*wide), *small)


def line_kernel(got_ref, out_ref):
    half = got_ref.shape[0] // 2
    line = jnp.concatenate([jnp.sum(got_ref[:half], 0), jnp.sum(got_ref[half:], 0)], 0)
    for k in range(out_ref.shape[0]):
        out_ref[k] = line


def line_of(got, count):
    return pl.pallas_call(
        line_kernel,
        out_shape=pltpu.VMEM((count, 32, 128), jnp.float32),
        in_specs=[VECTOR],
        out_specs=VECTOR,
        cost_estimate=pl.CostEstimate(flops=5_000_000_000, bytes_accessed=1024, transcendentals=0),
    )(*near(got))


def total_kernel(odd_ref, got_ref, out_ref):
    total = jnp.sum(got_ref[...], 0)
    odd = odd_ref[0] == 1
    own = jnp.where(odd, total[16:], total[:16])
    ahead = jnp.where(odd, total[:16], total[16:])
    for n, block in enumerate((own, ahead)):
        for k in range(2):
            rows = [block[:, 64 * k + 32 * r : 64 * k + 32 * r + 32] for r in range(2)]
            out_ref[:, 64 * n + 32 * k : 64 * n + 32 * k + 32] = jnp.concatenate(rows, 0)


def total_of(odd, got):
    return pl.pallas_call(
        total_kernel,
        out_shape=pltpu.VMEM((32, 128), jnp.float32),
        in_specs=[SCALAR, VECTOR],
        out_specs=VECTOR,
        cost_estimate=pl.CostEstimate(
            flops=100_000, bytes_accessed=1024, transcendentals=0
        ),
    )(odd, *near(got))


def finish_kernel(
    odd_ref, inter_ref, psi_ref, odd1_ref, even1_ref, odd2_ref, even2_ref, odd3_ref, even3_ref, h_ref,
    out_ref, wide, made, into, out
):
    steps = out.shape[0]
    step = made.shape[1] // steps
    spans = [pl.ds(k * step, step) for k in range(steps)]

    def finish(*refs):
        loads = [
            [
                pltpu.make_async_copy(ref.at[:, at], wide.at[n, :, at], into.at[k, n])
                for n, ref in enumerate(refs)
            ]
            for k, at in enumerate(spans)
        ]
        for load in loads:
            for copy in load:
                copy.start()
        inter = inter_ref[...]
        stores = []
        for k, at in enumerate(spans):
            for copy in loads[k]:
                copy.wait()
            window = jnp.concatenate([wide[n, :, at] for n in range(1, 5)], 0)
            made[:, at] = wide[0, :, at] - product(inter, window, ((1,), (0,)))
            stores.append(pltpu.make_async_copy(made.at[:, at], out_ref.at[:, at], out.at[k]))
            stores[-1].start()
        for copy in stores:
            copy.wait()

    @pl.when(odd_ref[0] == 0)
    def _():
        finish(h_ref, psi_ref, even2_ref, odd1_ref, odd3_ref)

    @pl.when(odd_ref[0] == 1)
    def _():
        finish(h_ref, psi_ref, odd2_ref, even1_ref, even3_ref)


def finished(odd, inter, blocks, hpsi):
    shape = hpsi.shape
    return pl.pallas_call(
        finish_kernel,
        out_shape=jax.ShapeDtypeStruct(shape, jnp.float32),
        in_specs=[SCALAR, VECTOR] + [ANYWHERE] * 8,
        out_specs=ANYWHERE,
        scratch_shapes=[
            pltpu.VMEM((5,) + shape, jnp.float32),
            pltpu.VMEM(shape, jnp.float32),
            pltpu.SemaphoreType.DMA((6, 5)),
            pltpu.SemaphoreType.DMA((6,)),
        ],
        compiler_params=PARAMS,
    )(odd, *near(inter, *blocks), hpsi)


def on_device(psi, hpsi):
    odd = lax.axis_index("core").astype(jnp.int32).reshape(1)
    odd2 = shifted(psi, 2, 1, 2)
    ahead1 = shifted(hpsi, -1)
    own, own_odd = overlap(hpsi, psi), overlap(hpsi, odd2)
    psi_later, own, own_odd = lax.optimization_barrier((psi, own, own_odd))
    even2 = shifted(psi_later, 2, 0, 2)

    ahead, ahead_odd = overlap(ahead1, psi), overlap(ahead1, odd2)
    even1 = lax.ppermute(psi, "core", [(0, 1)])
    for_next, even1 = lax.optimization_barrier((jnp.concatenate([ahead, ahead_odd], 1), even1))
    hopped = shifted(for_next, 2, 1, 2)

    slots = slots_of(
        odd, (hpsi, ahead1, even2), (own, ahead, own_odd, hopped), 2 * lax.axis_size("x")
    )
    slots, odd2_later, even2_later = lax.optimization_barrier((slots, odd2, even2))
    got = lax.all_to_all(slots, ("core", "x"), 0, 0, tiled=True)
    odd3 = shifted(odd2_later, 1, 1, 2)
    odd1 = lax.ppermute(odd2_later, "core", [(1, 0)])
    even3 = lax.ppermute(even2_later, "core", [(0, 1)])
    line = line_of(got, lax.axis_size("zh"))
    got = lax.all_to_all(line, "zh", 0, 0, tiled=True)
    inter = total_of(odd, got)
    return finished(odd, inter, (psi, odd1, even1, odd2, even2, odd3, even3), hpsi)


def solution(mesh):
    sizes = {"zl": 2, "y": 8, "core": 2, "zh": 4, "x": 8}
    fine = Mesh(mesh.devices.reshape(tuple(sizes.values())), tuple(sizes))
    placed = P(BAND, GA)
    return jax.shard_map(
        on_device, mesh=fine, in_specs=(placed, placed), out_specs=placed, check_vma=False
    )
```
